32 devices in a mesh: box: 4 (over x, core), dir: 8 (over z, y).
Axes of the slice: x: 2, y: 2, z: 4, core: 2. Of those that a mesh axis runs over, the one named last changes fastest.
Arguments:
- fine_pattern: bfloat16 [128, 2, 16, 8192], P(('box', 'dir')), may hold values from -6 to 6
- fine_interp: bfloat16 [32, 384, 896], P('dir'), may hold values from -0.3125 to 0.3125
- mid_interp: bfloat16 [32, 1024, 3328], P('dir'), may hold values from -0.1875 to 0.1875
- fine_angle: float32 [8, 28672], P(None, 'dir'), may hold values from -3.140625 to 3.140625
- top_angle: float32 [8, 106496], P(None, 'dir'), may hold values from -3.140625 to 3.140625
- translator: bfloat16 [64, 2, 106496], P(None, None, 'dir'), may hold values from -1 to 1
- fine_position: int32 [128], replicated, may hold values from 0 to 7
- mid_position: int32 [32], replicated, may hold values from 0 to 7
- fine_parent: int32 [128], replicated, may hold values from 0 to 31, as said below
- mid_parent: int32 [32], replicated, may hold values from 0 to 7, as said below
- pair_target: int32 [64], replicated, may hold values from 0 to 7
- pair_source: int32 [64], replicated, may hold values from 0 to 7
- pair_kind: int32 [64], replicated, may hold values from 0 to 63
Outputs:
- top_incoming: float32 [8, 2, 16, 106496], P('box', None, None, 'dir')
- mid_incoming: float32 [32, 2, 16, 28672], P('box', None, None, 'dir')
The draws below stay inside these ranges and needn't reach their ends.
Inputs may be any that keep to these rules, and one draw needn't show every extreme that they name: `fine_parent`: for every k, the fine boxes k * 32 to (k + 1) * 32 - 1 have their parents among the middle boxes k * 8 to (k + 1) * 8 - 1, and every middle box has exactly 4 children. `mid_parent`: for every k, the middle boxes k * 8 to (k + 1) * 8 - 1 have their parents among the top boxes k * 2 to (k + 1) * 2 - 1, and every top box has exactly 4 children.
All inputs are finite; a program needn't handle non-finite values.
Results may differ from the reference program's by a relative error of at most 0.0072.
Values may be sent and summed in bfloat16 or wider, within the bound.
A program may use at most 128 MiB of HBM per device.

```python
import jax
import jax.numpy as jnp
from jax import lax

RHS = 16
SECT = 32
FS = 256
MS = 896
TS = 3328
HALO = 64
POS = 8
KINDS = 64
FGROUP = 32
MGROUP = 8
FBOX = 128
MBOX = 32
TBOX = 8
FDIR = 8192
MDIR = 28672
TDIR = 106496
PAIRS = 64


def grouped_parents(key, count_all, per_group):
    groups = count_all // per_group
    group_keys = jax.random.split(key, groups)
    shuffled = jax.vmap(lambda single: jax.random.permutation(single, per_group))(group_keys)
    offsets = jnp.arange(groups, dtype=jnp.int32)[:, None] * (per_group // 4)
    return (offsets + shuffled.astype(jnp.int32) // 4).reshape(count_all).astype(jnp.int32)


def draw_fine_parent(key, part):
    return grouped_parents(jax.random.fold_in(key, 17), FBOX, FGROUP)


def draw_mid_parent(key, part):
    return grouped_parents(jax.random.fold_in(key, 29), MBOX, MGROUP)


def with_ends(values, key, low, largest):
    dims = values.shape
    index_at = [jax.random.randint(jax.random.fold_in(key, axis), (), 0, dims[axis]) for axis in range(len(dims))]
    values = values.at[tuple(index_at)].set(low)
    longest = dims.index(max(dims))
    index_at[longest] = (index_at[longest] + 1) % dims[longest]
    return values.at[tuple(index_at)].set(largest)


def level_of(key, shape, cuts, smallest, high):
    loudness, own = 1.0, jax.random.fold_in(key, 6)
    for position, blocks in cuts:
        steps = jnp.exp(jax.random.uniform(jax.random.fold_in(own, position), (blocks,), jnp.float32, smallest / len(cuts), high / len(cuts)))
        loudness = loudness * jnp.repeat(steps, shape[position] // blocks).reshape([-1 if axis == position else 1 for axis in range(len(shape))])
    return loudness


def normal_values(rng, shape, scale, bound, cuts=(), kind=jnp.bfloat16):
    drawn = jax.random.normal(rng, shape, jnp.float32) * scale
    if len(cuts) > 0:
        drawn = level_of(rng, shape, cuts, -0.22, 0.18) * drawn
    return jnp.clip(drawn, min=-bound, max=bound).astype(kind)


def setup_inputs(seed: int = 0) -> dict:
    key_of = jax.random.split(jax.random.key(seed), 14)
    fine_pattern = normal_values(key_of[0], (FBOX, 2, RHS, FDIR), 1.0, 6.0, ((0, 32),))
    fine_interp = normal_values(key_of[1], (SECT, FS + 2 * HALO, MS), (FS + 2 * HALO) ** -0.5, 0.3125, ((0, 8),))
    mid_interp = normal_values(key_of[2], (SECT, MS + 2 * HALO, TS), (MS + 2 * HALO) ** -0.5, 0.1875, ((0, 8),))
    fine_angle = jnp.clip(jax.random.uniform(key_of[3], (POS, MDIR), jnp.float32, -3.140625, 3.140625), -3.140625, 3.140625)
    top_angle = jnp.clip(jax.random.uniform(key_of[4], (POS, TDIR), jnp.float32, -3.140625, 3.140625), -3.140625, 3.140625)
    translator = normal_values(key_of[5], (KINDS, 2, TDIR), 0.15, 1.0, ((2, 8),))
    fine_position = with_ends(jax.random.randint(key_of[6], (FBOX,), 0, POS), jax.random.fold_in(key_of[6], 1), 0, POS - 1).astype(jnp.int32)
    mid_position = with_ends(jax.random.randint(key_of[7], (MBOX,), 0, POS), jax.random.fold_in(key_of[7], 1), 0, POS - 1).astype(jnp.int32)
    fine_parent = draw_fine_parent(jax.random.fold_in(key_of[13], 71), 0)
    mid_parent = draw_mid_parent(jax.random.fold_in(key_of[13], 71), 0)
    pair_target = with_ends(jax.random.randint(key_of[10], (PAIRS,), 0, TBOX), jax.random.fold_in(key_of[10], 1), 0, TBOX - 1).astype(jnp.int32)
    pair_source = with_ends(jax.random.randint(key_of[11], (PAIRS,), 0, TBOX), jax.random.fold_in(key_of[11], 1), 0, TBOX - 1).astype(jnp.int32)
    pair_kind = with_ends(jax.random.randint(key_of[12], (PAIRS,), 0, KINDS), jax.random.fold_in(key_of[12], 1), 0, KINDS - 1).astype(jnp.int32)
    return dict(fine_pattern=fine_pattern, fine_interp=fine_interp, mid_interp=mid_interp, fine_angle=fine_angle, top_angle=top_angle, translator=translator, fine_position=fine_position, mid_position=mid_position, fine_parent=fine_parent, mid_parent=mid_parent, pair_target=pair_target, pair_source=pair_source, pair_kind=pair_kind)


def extended(pattern, width):
    shape = pattern.shape[:-1] + (SECT, width)
    blocks = pattern.reshape(shape)
    leading = jnp.roll(pattern, HALO, axis=-1).reshape(shape)[..., :HALO]
    trailing = jnp.roll(pattern, -HALO, axis=-1).reshape(shape)[..., width - HALO:]
    return jnp.concatenate([leading, blocks, trailing], axis=-1)


def settle(values):
    return lax.optimization_barrier(values.astype(jnp.bfloat16))


def rotate(pattern, angles):
    cosine = jnp.cos(angles)[:, None, :]
    sine = jnp.sin(angles)[:, None, :]
    real_part = pattern[:, 0]
    imag_part = pattern[:, 1]
    return jnp.stack([cosine * real_part - sine * imag_part, sine * real_part + cosine * imag_part], axis=1)


def translate(coupling, sources):
    highest = lax.Precision.HIGHEST
    real_part = jnp.einsum("tud,urd->trd", coupling[:, :, 0], sources[:, 0], precision=highest) - jnp.einsum("tud,urd->trd", coupling[:, :, 1], sources[:, 1], precision=highest)
    imag_part = jnp.einsum("tud,urd->trd", coupling[:, :, 0], sources[:, 1], precision=highest) + jnp.einsum("tud,urd->trd", coupling[:, :, 1], sources[:, 0], precision=highest)
    return jnp.stack([real_part, imag_part], axis=1)


def reference(fine_pattern, fine_interp, mid_interp, fine_angle, top_angle, translator, fine_position, mid_position, fine_parent, mid_parent, pair_target, pair_source, pair_kind):
    highest = lax.Precision.HIGHEST
    widened_fine = jnp.moveaxis(extended(fine_pattern, FS), 3, 0)
    fine_table = jnp.moveaxis(fine_angle.reshape(POS, SECT, MS), 1, 0)

    def fine_step(inputs):
        widened, matrix, angle_table = inputs
        coarse = settle(jnp.einsum("bcrk,kn->bcrn", widened.astype(jnp.float32), matrix.astype(jnp.float32), precision=highest))
        turned = rotate(coarse.astype(jnp.float32), angle_table[fine_position])
        return jax.ops.segment_sum(turned, fine_parent, num_segments=MBOX).astype(jnp.bfloat16)

    mid_sectors = lax.map(fine_step, (widened_fine, fine_interp, fine_table))
    mid_pattern = jnp.moveaxis(mid_sectors, 0, 3).reshape(MBOX, 2, RHS, MDIR)

    slot_index = pair_target * TBOX + pair_source
    onehot_pair = (slot_index[:, None] == jnp.arange(TBOX * TBOX, dtype=jnp.int32)[None, :]).astype(jnp.float32)
    onehot_kind = (pair_kind[:, None] == jnp.arange(KINDS, dtype=jnp.int32)[None, :]).astype(jnp.float32)
    counts = jnp.dot(onehot_pair.T, onehot_kind, precision=highest).astype(jnp.bfloat16)

    widened_mid = jnp.moveaxis(extended(mid_pattern, MS), 3, 0)
    top_table = jnp.moveaxis(top_angle.reshape(POS, SECT, TS), 1, 0)
    operators = jnp.moveaxis(translator.reshape(KINDS, 2, SECT, TS), 2, 0)

    def top_step(inputs):
        widened, matrix, angle_table, operator_table = inputs
        coarse = settle(jnp.einsum("bcrk,kn->bcrn", widened.astype(jnp.float32), matrix.astype(jnp.float32), precision=highest))
        angles = angle_table[mid_position]
        turned = rotate(coarse.astype(jnp.float32), angles)
        top_pattern = settle(jax.ops.segment_sum(turned, mid_parent, num_segments=TBOX))
        coupling = settle(jnp.dot(counts, operator_table.reshape(KINDS, 2 * TS), preferred_element_type=jnp.float32).reshape(TBOX, TBOX, 2, TS))
        incoming = translate(coupling.astype(jnp.float32), top_pattern.astype(jnp.float32))
        rounded = settle(incoming)
        spread = settle(rotate(rounded.astype(jnp.float32)[mid_parent], -angles))
        contrib = jnp.einsum("bcrn,kn->bcrk", spread.astype(jnp.float32), matrix.astype(jnp.float32), precision=highest)
        return incoming, contrib

    incoming, contrib = lax.map(top_step, (widened_mid, mid_interp, top_table, operators))
    top_incoming = jnp.moveaxis(incoming, 0, 3).reshape(TBOX, 2, RHS, TDIR)
    central = contrib[..., HALO:HALO + MS]
    leading = contrib[..., :HALO]
    trailing = contrib[..., HALO + MS:]
    central = central.at[..., :HALO].add(jnp.roll(trailing, 1, axis=0))
    central = central.at[..., MS - HALO:].add(jnp.roll(leading, -1, axis=0))
    mid_incoming = jnp.moveaxis(central, 0, 3).reshape(MBOX, 2, RHS, MDIR)
    return top_incoming, mid_incoming
```

```python
import functools

import jax
import jax.numpy as jnp
from jax import lax
from jax.experimental import pallas as pl
from jax.experimental.pallas import tpu as pltpu
from jax.sharding import PartitionSpec as P

MESH = pl.DeviceIdType.MESH
F32 = jnp.float32
BF16 = jnp.bfloat16
EDGE = 128


def visit_order(sectors):
    if sectors <= 2:
        return list(range(sectors))
    return list(range(1, sectors - 1)) + [0, sectors - 1]


def down_order(sectors):
    if sectors <= 2:
        return list(range(sectors))
    inner = list(range(1, sectors - 1))
    return inner[:1] + [0, sectors - 1] + inner[1:]


def kernel(
    fchild,
    mchild,
    mrank,
    fine,
    fint,
    mint,
    trans,
    fcos,
    fsin,
    tcos,
    tsin,
    cnt,
    top_out,
    mid_out,
    xf,
    fhl,
    fhr,
    wf,
    wm,
    xm,
    mhl,
    mhr,
    xs,
    gat,
    traw,
    tview,
    cpl,
    spread,
    acc,
    stage,
    esl,
    esr,
    erl,
    err,
    a2a_send,
    a2a_recv,
    own_sem,
    wf_sem,
    wm_sem,
    tr_sem,
    fh_send,
    fh_recv,
    mh_send,
    mh_recv,
    g_send,
    g_recv,
    ed_send,
    ed_recv,
    out_sem,
):
    nd = lax.axis_size("dir")
    nb = lax.axis_size("box")
    me = lax.axis_index("dir")
    box = lax.axis_index("box")
    chips = nb // 2
    sectors, kf, ms = fint.shape
    km, ts = mint.shape[1:]
    fl, _, rhs, fdir = fine.shape
    fg, _, _, fblock = xf.shape
    fs = fblock // sectors
    halo = (kf - fs) // 2
    mg = xm.shape[0]
    tg = mg // 4
    nt = tg * nb
    rows = 2 * rhs
    pad = EDGE - halo
    spanf = fs + 2 * EDGE
    spanm = ms + 2 * EDGE
    left = lax.rem(me + nd - 1, nd)
    right = lax.rem(me + 1, nd)
    sib = box + 1 - 2 * lax.rem(box, 2)
    across = [lax.rem(box + 2 * k, nb) for k in range(1, chips)]
    peers = [lax.rem(me + k, nd) for k in range(1, nd)]

    barrier = pltpu.get_barrier_semaphore()
    for p in peers:
        pl.semaphore_signal(barrier, inc=1, device_id={"dir": p}, device_id_type=MESH)
    for p in [sib] + across:
        pl.semaphore_signal(barrier, inc=1, device_id={"box": p}, device_id_type=MESH)
    pl.semaphore_wait(barrier, len(peers) + 1 + len(across))

    def columns(d):
        return pl.ds(pl.multiple_of(d * fblock, 128), fblock)

    mine = pl.ds(me * fl, fl)
    a2a = [
        pltpu.make_async_remote_copy(
            src_ref=fine.at[:, :, :, columns(p)],
            dst_ref=xf.at[mine],
            send_sem=a2a_send.at[k],
            recv_sem=a2a_recv.at[k],
            device_id={"dir": p},
            device_id_type=MESH,
        )
        for k, p in enumerate(peers)
    ]
    for c in a2a:
        c.start()
    own = pltpu.make_async_copy(fine.at[:, :, :, columns(me)], xf.at[mine], own_sem)
    own.start()

    wf_copies = [
        pltpu.make_async_copy(fint.at[s], wf.at[s, pl.ds(pad, kf)], wf_sem.at[s])
        for s in range(sectors)
    ]
    wm_copies = [
        pltpu.make_async_copy(mint.at[s], wm.at[s, pl.ds(pad, km)], wm_sem.at[s])
        for s in range(sectors)
    ]
    for c in wf_copies + wm_copies:
        c.start()

    for s in range(sectors):
        for buf, k, n in ((wf, kf, ms), (wm, km, ts)):
            buf[s, pl.ds(0, pad), :] = jnp.zeros((pad, n), BF16)
            buf[s, pl.ds(pad + k, pad), :] = jnp.zeros((pad, n), BF16)
    acc[...] = jnp.zeros(acc.shape, F32)

    kinds = trans.shape[0]
    for s in range(sectors):
        fetch = pltpu.make_async_copy(
            trans.at[:, :, pl.ds(s * ts, ts)], traw, tr_sem.at[s]
        )
        fetch.start()
        fetch.wait()

        @pl.loop(0, kinds // 8)
        def _(g, s=s):
            group = [traw[g * 8 + i].astype(F32) for i in range(8)]
            tview[
                pl.ds(pl.multiple_of(g * 16, 16), 16), pl.ds(s * ts, ts)
            ] = jnp.concatenate(group, axis=0).astype(BF16)

    own.wait()
    for c in a2a:
        c.wait_recv()

    def neighbour_copies(src_l, src_r, dst_l, dst_r, send, recv):
        return [
            pltpu.make_async_remote_copy(
                src_ref=src_r,
                dst_ref=dst_l,
                send_sem=send.at[0],
                recv_sem=recv.at[0],
                device_id={"dir": right},
                device_id_type=MESH,
            ),
            pltpu.make_async_remote_copy(
                src_ref=src_l,
                dst_ref=dst_r,
                send_sem=send.at[1],
                recv_sem=recv.at[1],
                device_id={"dir": left},
                device_id_type=MESH,
            ),
        ]

    fine_edges = neighbour_copies(
        xf.at[:, :, :, pl.ds(0, EDGE)],
        xf.at[:, :, :, pl.ds(fblock - EDGE, EDGE)],
        fhl,
        fhr,
        fh_send,
        fh_recv,
    )
    for c in fine_edges:
        c.start()

    def window(core, low, high, index, s, width):
        begin = s * width - EDGE
        end = (s + 1) * width + EDGE
        total = core.shape[3]
        parts = []
        if begin < 0:
            parts.append(low[index])
        first, last = max(begin, 0), min(end, total)
        parts.append(core[index, :, :, pl.ds(first, last - first)])
        if end > total:
            parts.append(high[index])
        parts = [p.reshape(rows, p.shape[-1]) for p in parts]
        return parts[0] if len(parts) == 1 else jnp.concatenate(parts, axis=1)

    halo_seen = False
    for s in visit_order(sectors):
        if (s == 0 or s == sectors - 1) and not halo_seen:
            for c in fine_edges:
                c.wait_recv()
            halo_seen = True
        wf_copies[s].wait()

        @pl.loop(0, mg)
        def _(m, s=s):
            gathered = jnp.concatenate(
                [window(xf, fhl, fhr, fchild[m * 4 + j], s, fs) for j in range(4)], axis=0
            )
            coarse = jnp.dot(gathered, wf[s], preferred_element_type=F32)
            coarse = coarse.astype(BF16).astype(F32)
            re = im = None
            for j in range(4):
                turn = pl.ds(m * 4 + j, 1)
                c = fcos[turn, pl.ds(s * ms, ms)]
                d = fsin[turn, pl.ds(s * ms, ms)]
                u = coarse[j * rows : j * rows + rhs]
                v = coarse[j * rows + rhs : (j + 1) * rows]
                a, b = c * u - d * v, d * u + c * v
                re, im = (a, b) if re is None else (re + a, im + b)
            xm[m, 0, :, pl.ds(s * ms, ms)] = re.astype(BF16)
            xm[m, 1, :, pl.ds(s * ms, ms)] = im.astype(BF16)

    mblock = sectors * ms
    mid_edges = neighbour_copies(
        xm.at[:, :, :, pl.ds(0, EDGE)],
        xm.at[:, :, :, pl.ds(mblock - EDGE, EDGE)],
        mhl,
        mhr,
        mh_send,
        mh_recv,
    )
    for c in mid_edges:
        c.start()

    tile = 256 if ts % 256 == 0 else 128
    tiles = ts // tile

    def near(s):
        return pltpu.make_async_remote_copy(
            src_ref=gat.at[s, box],
            dst_ref=gat.at[s, box],
            send_sem=g_send.at[s, 0],
            recv_sem=g_recv.at[s, 0],
            device_id={"box": sib},
            device_id_type=MESH,
        )

    def far(s, k):
        return pltpu.make_async_remote_copy(
            src_ref=gat.at[s, box],
            dst_ref=gat.at[s, box],
            send_sem=g_send.at[s, 1 + k],
            recv_sem=g_recv.at[s, 1 + k],
            device_id={"box": across[k]},
            device_id_type=MESH,
        )

    def pass_on(s, k):
        origin = lax.rem(box + nb - 2 * (k + 1), nb)
        return pltpu.make_async_remote_copy(
            src_ref=gat.at[s, origin],
            dst_ref=gat.at[s, origin],
            send_sem=g_send.at[s, chips + k],
            recv_sem=g_recv.at[s, chips + k],
            device_id={"box": sib},
            device_id_type=MESH,
        )

    halo_seen = False
    for s in visit_order(sectors):
        if (s == 0 or s == sectors - 1) and not halo_seen:
            for c in mid_edges:
                c.wait_recv()
            halo_seen = True
        wm_copies[s].wait()

        @pl.loop(0, mg)
        def _(i, s=s):
            xs[pl.ds(pl.multiple_of(i * rows, rows), rows), :] = window(
                xm, mhl, mhr, mchild[i], s, ms
            )

        @pl.loop(0, tiles)
        def _(n, s=s):
            here = pl.ds(pl.multiple_of(n * tile, tile), tile)
            whole = pl.ds(pl.multiple_of(s * ts + n * tile, 128), tile)
            coarse = jnp.dot(xs[...], wm[s, :, here], preferred_element_type=F32)
            coarse = coarse.astype(BF16).astype(F32)
            for t in range(tg):
                re = im = None
                for j in range(4):
                    i = t * 4 + j
                    turn = pl.ds(i, 1)
                    c = tcos[turn, whole]
                    d = tsin[turn, whole]
                    u = coarse[i * rows : i * rows + rhs]
                    v = coarse[i * rows + rhs : (i + 1) * rows]
                    a, b = c * u - d * v, d * u + c * v
                    re, im = (a, b) if re is None else (re + a, im + b)
                gat[s, box, t, 0, :, here] = re.astype(BF16)
                gat[s, box, t, 1, :, here] = im.astype(BF16)

        for k in range(chips - 1):
            far(s, k).start()
        near(s).start()

    order = down_order(sectors)
    edge_copies = neighbour_copies(esl, esr, erl, err, ed_send, ed_recv)
    out_copies = []
    for step, s in enumerate(order):
        for k in range(chips - 1):
            far(s, k).wait_recv()
            pass_on(s, k).start()
        near(s).wait_recv()
        for k in range(chips - 1):
            pass_on(s, k).wait_recv()
        slot = step % 2
        if step >= 2:
            out_copies[step - 2].wait()

        @pl.loop(0, tiles)
        def _(n, s=s, slot=slot):
            here = pl.ds(pl.multiple_of(n * tile, tile), tile)
            whole = pl.ds(pl.multiple_of(s * ts + n * tile, 128), tile)
            product = jnp.dot(cnt[...], tview[:, whole], preferred_element_type=F32)
            cpl[...] = product.astype(BF16).astype(F32)
            for t in range(tg):

                def add(u, total, t=t):
                    re, im = total
                    origin = u // tg
                    q = u - origin * tg
                    c = cpl[pl.ds(2 * (t * nt + u), 1), :]
                    d = cpl[pl.ds(2 * (t * nt + u) + 1, 1), :]
                    a = gat[s, origin, q, 0, :, here].astype(F32)
                    b = gat[s, origin, q, 1, :, here].astype(F32)
                    return re + (c * a - d * b), im + (c * b + d * a)

                total = (jnp.zeros((rhs, tile), F32), jnp.zeros((rhs, tile), F32))
                if nt <= 8:
                    for u in range(nt):
                        total = add(u, total)
                else:
                    total = lax.fori_loop(0, nt, add, total)
                re, im = total
                stage[slot, t, 0, :, here] = re
                stage[slot, t, 1, :, here] = im
                re = re.astype(BF16).astype(F32)
                im = im.astype(BF16).astype(F32)
                for j in range(4):
                    i = t * 4 + j
                    turn = pl.ds(i, 1)
                    c = tcos[turn, whole]
                    d = tsin[turn, whole]
                    spread[pl.ds(i * rows, rhs), :] = (c * re + d * im).astype(BF16)
                    spread[pl.ds(i * rows + rhs, rhs), :] = (c * im - d * re).astype(BF16)
            acc[:, :, pl.ds(s * ms, spanm)] += lax.dot_general(
                spread[...],
                wm[s, :, here],
                (((1,), (1,)), ((), ())),
                preferred_element_type=F32,
            ).reshape(mg, rows, spanm)

        out = pltpu.make_async_copy(
            stage.at[slot],
            top_out.at[:, :, :, pl.ds(s * ts, ts)],
            out_sem.at[step],
        )
        out.start()
        out_copies.append(out)
        if set(order[: step + 1]) >= {0, sectors - 1} and not (
            set(order[:step]) >= {0, sectors - 1}
        ):
            esl[...] = acc[:, :, pl.ds(0, EDGE)].astype(BF16)
            esr[...] = acc[:, :, pl.ds(EDGE + mblock, EDGE)].astype(BF16)
            for c in edge_copies:
                c.start()

    for c in edge_copies:
        c.wait_recv()
    acc[:, :, pl.ds(EDGE, EDGE)] += erl[...].astype(F32)
    acc[:, :, pl.ds(mblock, EDGE)] += err[...].astype(F32)

    @pl.loop(0, mg)
    def _(m):
        got = acc[mrank[m], :, pl.ds(EDGE, mblock)]
        mid_out[m] = got.reshape(2, rhs, mblock)

    for c in out_copies[-2:]:
        c.wait()
    for c in a2a + fine_edges + mid_edges + edge_copies:
        c.wait_send()
    for s in range(sectors):
        near(s).wait_send()
        for k in range(chips - 1):
            far(s, k).wait_send()
            pass_on(s, k).wait_send()


def ranking(parents, positions):
    count = parents.shape[0]
    index = jnp.arange(count, dtype=jnp.int32)
    before = (parents[None, :] < parents[:, None]) | (
        (parents[None, :] == parents[:, None]) & (index[None, :] < index[:, None])
    )
    rank = jnp.sum(before.astype(jnp.int32), axis=1)
    chosen = (rank[None, :] == index[:, None]).astype(jnp.int32)
    child = jnp.sum(chosen * index[None, :], axis=1)
    return rank, child, jnp.sum(chosen * positions[None, :], axis=1)


def pair_counts(
    pair_target, pair_source, pair_kind, target_base, target_count, source_count, kind_count
):
    inside = (pair_target >= target_base) & (pair_target < target_base + target_count)
    slot_index = jnp.where(inside, (pair_target - target_base) * source_count + pair_source, -1)
    onehot_pair = (
        slot_index[:, None] == jnp.arange(target_count * source_count, dtype=jnp.int32)[None, :]
    ).astype(BF16)
    onehot_kind = (pair_kind[:, None] == jnp.arange(kind_count, dtype=jnp.int32)[None, :]).astype(
        BF16
    )
    return jnp.dot(onehot_pair.T, onehot_kind, preferred_element_type=F32).astype(BF16)


def per_device(
    fine_pattern,
    fine_interp,
    mid_interp,
    fine_angle,
    top_angle,
    translator,
    fine_position,
    mid_position,
    fine_parent,
    mid_parent,
    pair_target,
    pair_source,
    pair_kind,
):
    box = lax.axis_index("box")
    nd = lax.axis_size("dir")
    nb = lax.axis_size("box")
    fl, _, rhs, fdir = fine_pattern.shape
    sectors, kf, ms = fine_interp.shape
    km, ts = mid_interp.shape[1:]
    kinds = translator.shape[0]
    fg = fl * nd
    mg = fg // 4
    tg = mg // 4
    nt = tg * nb
    rows = 2 * rhs
    fblock = fdir // nd
    fs = fblock // sectors
    mblock = sectors * ms
    tblock = sectors * ts
    chips = nb // 2
    tile = 256 if ts % 256 == 0 else 128

    def local(array, count):
        return lax.dynamic_slice_in_dim(array, box * count, count)

    _, fchild, fposc = ranking(local(fine_parent, fg), local(fine_position, fg))
    mrank, mchild, mposc = ranking(local(mid_parent, mg), local(mid_position, mg))
    fine_turns = fine_angle[fposc]
    top_turns = top_angle[mposc]
    counts = pair_counts(pair_target, pair_source, pair_kind, box * tg, tg, nt, kinds)
    eye = jnp.eye(2, dtype=BF16)
    cnt = (counts[:, None, :, None] * eye[None, :, None, :]).reshape(tg * nt * 2, kinds * 2)

    vmem = pl.BlockSpec(memory_space=pltpu.VMEM)
    smem = pl.BlockSpec(memory_space=pltpu.SMEM)
    hbm = pl.BlockSpec(memory_space=pl.ANY)
    dma = pltpu.SemaphoreType.DMA
    paths = 2 * chips - 1
    return pl.pallas_call(
        kernel,
        out_shape=(
            jax.ShapeDtypeStruct((tg, 2, rhs, tblock), F32),
            jax.ShapeDtypeStruct((mg, 2, rhs, mblock), F32),
        ),
        in_specs=[smem] * 3 + [hbm] * 4 + [vmem] * 5,
        out_specs=(hbm, vmem),
        scratch_shapes=[
            pltpu.VMEM((fg, 2, rhs, fblock), BF16),
            pltpu.VMEM((fg, 2, rhs, EDGE), BF16),
            pltpu.VMEM((fg, 2, rhs, EDGE), BF16),
            pltpu.VMEM((sectors, fs + 2 * EDGE, ms), BF16),
            pltpu.VMEM((sectors, ms + 2 * EDGE, ts), BF16),
            pltpu.VMEM((mg, 2, rhs, mblock), BF16),
            pltpu.VMEM((mg, 2, rhs, EDGE), BF16),
            pltpu.VMEM((mg, 2, rhs, EDGE), BF16),
            pltpu.VMEM((mg * rows, ms + 2 * EDGE), BF16),
            pltpu.VMEM((sectors, nb, tg, 2, rhs, ts), BF16),
            pltpu.VMEM((kinds, 2, ts), BF16),
            pltpu.VMEM((2 * kinds, tblock), BF16),
            pltpu.VMEM((tg * nt * 2, tile), F32),
            pltpu.VMEM((mg * rows, tile), BF16),
            pltpu.VMEM((mg, rows, mblock + 2 * EDGE), F32),
            pltpu.VMEM((2, tg, 2, rhs, ts), F32),
            pltpu.VMEM((mg, rows, EDGE), BF16),
            pltpu.VMEM((mg, rows, EDGE), BF16),
            pltpu.VMEM((mg, rows, EDGE), BF16),
            pltpu.VMEM((mg, rows, EDGE), BF16),
            dma((nd - 1,)),
            dma((nd - 1,)),
            dma,
            dma((sectors,)),
            dma((sectors,)),
            dma((sectors,)),
            dma((2,)),
            dma((2,)),
            dma((2,)),
            dma((2,)),
            dma((sectors, paths)),
            dma((sectors, paths)),
            dma((2,)),
            dma((2,)),
            dma((sectors,)),
        ],
        compiler_params=pltpu.CompilerParams(
            collective_id=0, has_side_effects=True, vmem_limit_bytes=63 * 1024 * 1024
        ),
    )(
        fchild,
        mchild,
        mrank,
        fine_pattern,
        fine_interp,
        mid_interp,
        translator,
        jnp.cos(fine_turns),
        jnp.sin(fine_turns),
        jnp.cos(top_turns),
        jnp.sin(top_turns),
        cnt,
    )


def solution(mesh):
    placed = (
        P(("box", "dir"), None, None, None),
        P("dir", None, None),
        P("dir", None, None),
        P(None, "dir"),
        P(None, "dir"),
        P(None, None, "dir"),
        P(),
        P(),
        P(),
        P(),
        P(),
        P(),
        P(),
    )
    return jax.shard_map(
        per_device,
        mesh=mesh,
        in_specs=placed,
        out_specs=(P("box", None, None, "dir"), P("box", None, None, "dir")),
        check_vma=False,
    )
```

```python
import functools

import jax
import jax.numpy as jnp
from jax import lax
from jax.experimental import pallas as pl
from jax.experimental.pallas import tpu as pltpu
from jax.sharding import PartitionSpec as P

MESH = pl.DeviceIdType.MESH
F32 = jnp.float32
BF16 = jnp.bfloat16
EDGE = 128


def visit_order(sectors):
    if sectors <= 2:
        return list(range(sectors))
    return [1, 0, sectors - 1] + list(range(2, sectors - 1))


def circle(angle):
    quarter = angle * 0.25
    x = quarter * quarter
    sine = quarter * (
        1.0 + x * (-1.0 / 6 + x * (1.0 / 120 + x * (-1.0 / 5040 + x * (1.0 / 362880))))
    )
    cosine = 1.0 + x * (
        -0.5 + x * (1.0 / 24 + x * (-1.0 / 720 + x * (1.0 / 40320 - x * (1.0 / 3628800))))
    )
    for _ in range(2):
        sine, cosine = 2.0 * sine * cosine, 1.0 - 2.0 * sine * sine
    return cosine, sine


def kernel(
    child,
    rank,
    fine,
    fint,
    mint,
    trans,
    fang,
    tang,
    fpos,
    mpos,
    cnt,
    top_out,
    mid_out,
    fcos,
    fsin,
    tcos,
    tsin,
    xf,
    fhl,
    fhr,
    wf,
    wm,
    xm,
    mhl,
    mhr,
    xs,
    gat,
    traw,
    tview,
    cpl,
    turned,
    spread,
    acc,
    stage,
    esl,
    esr,
    erl,
    err,
    a2a_send,
    a2a_recv,
    own_sem,
    wf_sem,
    wm_sem,
    tr_sem,
    fh_send,
    fh_recv,
    mh_send,
    mh_recv,
    g_send,
    g_recv,
    ed_send,
    ed_recv,
    out_sem,
    mid_sem,
):
    nd = lax.axis_size("dir")
    nb = lax.axis_size("box")
    me = lax.axis_index("dir")
    box = lax.axis_index("box")
    chips = nb // 2
    sectors, kf, ms = fint.shape
    km, ts = mint.shape[1:]
    fl, _, rhs, fdir = fine.shape
    fg, _, _, fblock = xf.shape
    fs = fblock // sectors
    halo = (kf - fs) // 2
    mg = xm.shape[0]
    tg = mg // 4
    nt = tg * nb
    rows = 2 * rhs
    pad = EDGE - halo
    spanf = fs + 2 * EDGE
    spanm = ms + 2 * EDGE
    left = lax.rem(me + nd - 1, nd)
    right = lax.rem(me + 1, nd)
    sib = box + 1 - 2 * lax.rem(box, 2)
    across = [lax.rem(box + 2 * k, nb) for k in range(1, chips)]
    peers = [lax.rem(me + k, nd) for k in range(1, nd)]

    barrier = pltpu.get_barrier_semaphore()
    for p in peers:
        pl.semaphore_signal(barrier, inc=1, device_id={"dir": p}, device_id_type=MESH)
    for p in [sib] + across:
        pl.semaphore_signal(barrier, inc=1, device_id={"box": p}, device_id_type=MESH)
    pl.semaphore_wait(barrier, len(peers) + 1 + len(across))

    def columns(d):
        return pl.ds(pl.multiple_of(d * fblock, 128), fblock)

    mine = pl.ds(me * fl, fl)
    a2a = [
        pltpu.make_async_remote_copy(
            src_ref=fine.at[:, :, :, columns(p)],
            dst_ref=xf.at[mine],
            send_sem=a2a_send.at[k],
            recv_sem=a2a_recv.at[k],
            device_id={"dir": p},
            device_id_type=MESH,
        )
        for k, p in enumerate(peers)
    ]
    for c in a2a:
        c.start()
    own = pltpu.make_async_copy(fine.at[:, :, :, columns(me)], xf.at[mine], own_sem)
    own.start()

    wf_copies = [
        pltpu.make_async_copy(fint.at[s], wf.at[s, pl.ds(pad, kf)], wf_sem.at[s])
        for s in range(sectors)
    ]
    wm_copies = [
        pltpu.make_async_copy(mint.at[s], wm.at[s, pl.ds(pad, km)], wm_sem.at[s])
        for s in range(sectors)
    ]
    for c in wf_copies + wm_copies:
        c.start()

    for s in range(sectors):
        for buf, k, n in ((wf, kf, ms), (wm, km, ts)):
            buf[s, pl.ds(0, pad), :] = jnp.zeros((pad, n), BF16)
            buf[s, pl.ds(pad + k, pad), :] = jnp.zeros((pad, n), BF16)
    acc[...] = jnp.zeros(acc.shape, F32)

    kinds = trans.shape[0]
    for s in range(sectors):
        fetch = pltpu.make_async_copy(
            trans.at[:, :, pl.ds(s * ts, ts)], traw, tr_sem.at[s]
        )
        fetch.start()
        fetch.wait()

        @pl.loop(0, kinds // 8)
        def _(g, s=s):
            group = [traw[g * 8 + i].astype(F32) for i in range(8)]
            tview[
                pl.ds(pl.multiple_of(g * 16, 16), 16), pl.ds(s * ts, ts)
            ] = jnp.concatenate(group, axis=0).astype(BF16)

    for angles, places, cosines, sines, width in (
        (fang, fpos, fcos, fsin, 128),
        (tang, mpos, tcos, tsin, 256),
    ):

        @pl.loop(0, angles.shape[1] // width)
        def _(n, angles=angles, places=places, cosines=cosines, sines=sines, width=width):
            here = pl.ds(pl.multiple_of(n * width, width), width)
            table = angles[:, here]
            place = jnp.broadcast_to(places[...], (places.shape[0], width))
            angle = jnp.zeros(place.shape, F32)
            for p in range(table.shape[0]):
                row = jnp.broadcast_to(table[p : p + 1], place.shape)
                angle = jnp.where(place == p, row, angle)
            cosine, sine = circle(angle)
            cosines[:, here] = cosine
            sines[:, here] = sine

    own.wait()
    for c in a2a:
        c.wait_recv()

    def neighbour_copies(src_l, src_r, dst_l, dst_r, send, recv):
        return [
            pltpu.make_async_remote_copy(
                src_ref=src_r,
                dst_ref=dst_l,
                send_sem=send.at[0],
                recv_sem=recv.at[0],
                device_id={"dir": right},
                device_id_type=MESH,
            ),
            pltpu.make_async_remote_copy(
                src_ref=src_l,
                dst_ref=dst_r,
                send_sem=send.at[1],
                recv_sem=recv.at[1],
                device_id={"dir": left},
                device_id_type=MESH,
            ),
        ]

    fine_edges = neighbour_copies(
        xf.at[:, :, :, pl.ds(0, EDGE)],
        xf.at[:, :, :, pl.ds(fblock - EDGE, EDGE)],
        fhl,
        fhr,
        fh_send,
        fh_recv,
    )
    for c in fine_edges:
        c.start()

    def window(core, low, high, index, s, width):
        begin = s * width - EDGE
        end = (s + 1) * width + EDGE
        total = core.shape[3]
        parts = []
        if begin < 0:
            parts.append(low[index])
        first, last = max(begin, 0), min(end, total)
        parts.append(core[index, :, :, pl.ds(first, last - first)])
        if end > total:
            parts.append(high[index])
        parts = [p.reshape(rows, p.shape[-1]) for p in parts]
        return parts[0] if len(parts) == 1 else jnp.concatenate(parts, axis=1)

    group = 2 if mg % 2 == 0 else 1
    halo_seen = False
    for s in visit_order(sectors):
        if (s == 0 or s == sectors - 1) and not halo_seen:
            for c in fine_edges:
                c.wait_recv()
            halo_seen = True
        wf_copies[s].wait()

        @pl.loop(0, mg // group)
        def _(g, s=s):
            begin = g * 4 * group
            gathered = jnp.concatenate(
                [window(xf, fhl, fhr, child[begin + i], s, fs) for i in range(4 * group)], axis=0
            )
            coarse = jnp.dot(gathered, wf[s], preferred_element_type=F32)
            coarse = coarse.astype(BF16).astype(F32)
            for h in range(group):
                re = im = None
                for i in range(4 * h, 4 * h + 4):
                    turn = pl.ds(begin + i, 1)
                    c = fcos[turn, pl.ds(s * ms, ms)]
                    d = fsin[turn, pl.ds(s * ms, ms)]
                    u = coarse[i * rows : i * rows + rhs]
                    v = coarse[i * rows + rhs : (i + 1) * rows]
                    a, b = c * u - d * v, d * u + c * v
                    re, im = (a, b) if re is None else (re + a, im + b)
                xm[g * group + h, 0, :, pl.ds(s * ms, ms)] = re.astype(BF16)
                xm[g * group + h, 1, :, pl.ds(s * ms, ms)] = im.astype(BF16)

    mblock = sectors * ms
    mid_edges = neighbour_copies(
        xm.at[:, :, :, pl.ds(0, EDGE)],
        xm.at[:, :, :, pl.ds(mblock - EDGE, EDGE)],
        mhl,
        mhr,
        mh_send,
        mh_recv,
    )
    for c in mid_edges:
        c.start()

    tile = 256 if ts % 256 == 0 else 128
    tiles = ts // tile

    first = (tiles + 1) // 2
    halves = [(0, first)] + ([(first, tiles)] if first < tiles else [])

    def exchange(s, h, origin, path, target):
        low, high = halves[h]
        block = gat.at[s, origin, :, :, :, pl.ds(low * tile, (high - low) * tile)]
        return pltpu.make_async_remote_copy(
            src_ref=block,
            dst_ref=block,
            send_sem=g_send.at[2 * s + h, path],
            recv_sem=g_recv.at[2 * s + h, path],
            device_id={"box": target},
            device_id_type=MESH,
        )

    def near(s, h):
        return exchange(s, h, box, 0, sib)

    def far(s, h, k):
        return exchange(s, h, box, 1 + k, across[k])

    def pass_on(s, h, k):
        return exchange(s, h, lax.rem(box + nb - 2 * (k + 1), nb), chips + k, sib)

    halo_seen = False
    for s in visit_order(sectors):
        if (s == 0 or s == sectors - 1) and not halo_seen:
            for c in mid_edges:
                c.wait_recv()
            halo_seen = True
        wm_copies[s].wait()

        @pl.loop(0, mg)
        def _(i, s=s):
            xs[pl.ds(pl.multiple_of(i * rows, rows), rows), :] = window(
                xm, mhl, mhr, child[fg + i], s, ms
            )

        for h in range(len(halves)):

            @pl.loop(*halves[h])
            def _(n, s=s):
                here = pl.ds(pl.multiple_of(n * tile, tile), tile)
                whole = pl.ds(pl.multiple_of(s * ts + n * tile, 128), tile)
                coarse = jnp.dot(xs[...], wm[s, :, here], preferred_element_type=F32)
                coarse = coarse.astype(BF16).astype(F32)
                for t in range(tg):
                    re = im = None
                    for j in range(4):
                        i = t * 4 + j
                        turn = pl.ds(i, 1)
                        c = tcos[turn, whole]
                        d = tsin[turn, whole]
                        u = coarse[i * rows : i * rows + rhs]
                        v = coarse[i * rows + rhs : (i + 1) * rows]
                        a, b = c * u - d * v, d * u + c * v
                        re, im = (a, b) if re is None else (re + a, im + b)
                    gat[s, box, t, 0, :, here] = re.astype(BF16)
                    gat[s, box, t, 1, :, here] = im.astype(BF16)

            for k in range(chips - 1):
                far(s, h, k).start()
            near(s, h).start()

    order = visit_order(sectors)
    edge_copies = neighbour_copies(esl, esr, erl, err, ed_send, ed_recv)
    out_copies = []
    mfirst = rank.shape[0] - nb * mg + box * mg
    for step, s in enumerate(order):
        slot = step % 2
        if step >= 2:
            out_copies[step - 2].wait()
        for h in range(len(halves)):
            for k in range(chips - 1):
                far(s, h, k).wait_recv()
                pass_on(s, h, k).start()
            near(s, h).wait_recv()
            for k in range(chips - 1):
                pass_on(s, h, k).wait_recv()

            @pl.loop(*halves[h])
            def _(n, s=s, slot=slot):
                here = pl.ds(pl.multiple_of(n * tile, tile), tile)
                whole = pl.ds(pl.multiple_of(s * ts + n * tile, 128), tile)
                product = jnp.dot(cnt[...], tview[:, whole], preferred_element_type=F32)
                cpl[...] = product.astype(BF16).astype(F32)
                for t in range(tg):

                    def add(u, total, t=t):
                        re, im = total
                        origin = u // tg
                        q = u - origin * tg
                        c = cpl[pl.ds(2 * (t * nt + u), 1), :]
                        d = cpl[pl.ds(2 * (t * nt + u) + 1, 1), :]
                        a = gat[s, origin, q, 0, :, here].astype(F32)
                        b = gat[s, origin, q, 1, :, here].astype(F32)
                        return re + (c * a - d * b), im + (c * b + d * a)

                    total = (jnp.zeros((rhs, tile), F32), jnp.zeros((rhs, tile), F32))
                    if nt <= 8:
                        for u in range(nt):
                            total = add(u, total)
                    else:
                        total = lax.fori_loop(0, nt, add, total)
                    re, im = total
                    stage[slot, t, 0, :, here] = re
                    stage[slot, t, 1, :, here] = im
                    re = re.astype(BF16).astype(F32)
                    im = im.astype(BF16).astype(F32)
                    for j in range(4):
                        i = t * 4 + j
                        turn = pl.ds(i, 1)
                        c = tcos[turn, whole]
                        d = tsin[turn, whole]
                        turned[i, 0] = (c * re + d * im).astype(BF16)
                        turned[i, 1] = (c * im - d * re).astype(BF16)
                for m in range(mg):
                    spread[pl.ds(m * rows, rows), :] = turned[
                        rank[mfirst + m]
                    ].reshape(rows, tile)
                acc[:, :, :, pl.ds(s * ms, spanm)] += lax.dot_general(
                    spread[...],
                    wm[s, :, here],
                    (((1,), (1,)), ((), ())),
                    preferred_element_type=F32,
                ).reshape(mg, 2, rhs, spanm)

        out = pltpu.make_async_copy(
            stage.at[slot],
            top_out.at[:, :, :, pl.ds(s * ts, ts)],
            out_sem.at[step],
        )
        out.start()
        out_copies.append(out)
        if set(order[: step + 1]) >= {0, sectors - 1} and not (
            set(order[:step]) >= {0, sectors - 1}
        ):
            esl[...] = acc[:, :, :, pl.ds(0, EDGE)].astype(BF16)
            esr[...] = acc[:, :, :, pl.ds(EDGE + mblock, EDGE)].astype(BF16)
            for c in edge_copies:
                c.start()

    for c in edge_copies:
        c.wait_recv()
    acc[:, :, :, pl.ds(EDGE, EDGE)] += erl[...].astype(F32)
    acc[:, :, :, pl.ds(mblock, EDGE)] += err[...].astype(F32)
    mid_copy = pltpu.make_async_copy(
        acc.at[:, :, :, pl.ds(EDGE, mblock)], mid_out, mid_sem
    )
    mid_copy.start()
    mid_copy.wait()

    for c in out_copies[-2:]:
        c.wait()
    for c in a2a + fine_edges + mid_edges + edge_copies:
        c.wait_send()
    for s in range(sectors):
        for h in range(len(halves)):
            near(s, h).wait_send()
            for k in range(chips - 1):
                far(s, h, k).wait_send()
                pass_on(s, h, k).wait_send()


def ranking(parents, wanted, positions):
    index = jnp.arange(parents.shape[0], dtype=jnp.int32)
    before = (parents[None, :] < parents[:, None]) | (
        (parents[None, :] == parents[:, None]) & (index[None, :] < index[:, None])
    )
    rank = jnp.sum(before.astype(jnp.int32), axis=1)
    chosen = (rank[None, :] == wanted[:, None]).astype(jnp.int32)
    child = jnp.sum(chosen * index[None, :], axis=1)
    return rank, child, jnp.sum(chosen * positions[None, :], axis=1, keepdims=True)


def pair_counts(pair_target, pair_source, pair_kind, base, targets, sources, kinds):
    place = jnp.arange(targets * sources * 2, dtype=jnp.int32)
    column = jnp.arange(kinds * 2, dtype=jnp.int32)
    inside = (pair_target >= base) & (pair_target < base + targets)
    slot = jnp.where(inside, (pair_target - base) * sources + pair_source, -1)
    in_slot = (slot[None, :] == (place // 2)[:, None]).astype(BF16)
    of_kind = (pair_kind[:, None] == (column // 2)[None, :]).astype(BF16)
    counts = jnp.dot(in_slot, of_kind, preferred_element_type=F32)
    same = (place % 2)[:, None] == (column % 2)[None, :]
    return jnp.where(same, counts, 0.0).astype(BF16)


def per_device(
    fine_pattern,
    fine_interp,
    mid_interp,
    fine_angle,
    top_angle,
    translator,
    fine_position,
    mid_position,
    fine_parent,
    mid_parent,
    pair_target,
    pair_source,
    pair_kind,
):
    box = lax.axis_index("box")
    nd = lax.axis_size("dir")
    nb = lax.axis_size("box")
    fl, _, rhs, fdir = fine_pattern.shape
    sectors, kf, ms = fine_interp.shape
    km, ts = mid_interp.shape[1:]
    kinds = translator.shape[0]
    fg = fl * nd
    mg = fg // 4
    tg = mg // 4
    nt = tg * nb
    rows = 2 * rhs
    fblock = fdir // nd
    fs = fblock // sectors
    mblock = sectors * ms
    tblock = sectors * ts
    chips = nb // 2
    tile = 256 if ts % 256 == 0 else 128

    fine_all = fine_parent.shape[0]
    slots = jnp.arange(fg + mg, dtype=jnp.int32)
    start = jnp.where(slots < fg, box * fg, fine_all + box * mg - fg)
    rank, child, place = ranking(
        jnp.concatenate([fine_parent, mid_parent + fine_all]),
        slots + start,
        jnp.concatenate([fine_position, mid_position]),
    )
    index = jnp.arange(rank.shape[0], dtype=jnp.int32)
    inner = jnp.where(index < fine_all, index % fg, (index - fine_all) % mg)
    rank = rank - (index - inner)
    child = child - jnp.where(slots < fg, box * fg, fine_all + box * mg)
    cnt = pair_counts(pair_target, pair_source, pair_kind, box * tg, tg, nt, kinds)

    vmem = pl.BlockSpec(memory_space=pltpu.VMEM)
    smem = pl.BlockSpec(memory_space=pltpu.SMEM)
    hbm = pl.BlockSpec(memory_space=pl.ANY)
    dma = pltpu.SemaphoreType.DMA
    paths = 2 * chips - 1
    return pl.pallas_call(
        kernel,
        out_shape=(
            jax.ShapeDtypeStruct((tg, 2, rhs, tblock), F32),
            jax.ShapeDtypeStruct((mg, 2, rhs, mblock), F32),
        ),
        in_specs=[smem] * 2 + [hbm] * 4 + [vmem] * 5,
        out_specs=(hbm, hbm),
        scratch_shapes=[
            pltpu.VMEM((fg, mblock), F32),
            pltpu.VMEM((fg, mblock), F32),
            pltpu.VMEM((mg, tblock), F32),
            pltpu.VMEM((mg, tblock), F32),
            pltpu.VMEM((fg, 2, rhs, fblock), BF16),
            pltpu.VMEM((fg, 2, rhs, EDGE), BF16),
            pltpu.VMEM((fg, 2, rhs, EDGE), BF16),
            pltpu.VMEM((sectors, fs + 2 * EDGE, ms), BF16),
            pltpu.VMEM((sectors, ms + 2 * EDGE, ts), BF16),
            pltpu.VMEM((mg, 2, rhs, mblock), BF16),
            pltpu.VMEM((mg, 2, rhs, EDGE), BF16),
            pltpu.VMEM((mg, 2, rhs, EDGE), BF16),
            pltpu.VMEM((mg * rows, ms + 2 * EDGE), BF16),
            pltpu.VMEM((sectors, nb, tg, 2, rhs, ts), BF16),
            pltpu.VMEM((kinds, 2, ts), BF16),
            pltpu.VMEM((2 * kinds, tblock), BF16),
            pltpu.VMEM((tg * nt * 2, tile), F32),
            pltpu.VMEM((mg, 2, rhs, tile), BF16),
            pltpu.VMEM((mg * rows, tile), BF16),
            pltpu.VMEM((mg, 2, rhs, mblock + 2 * EDGE), F32),
            pltpu.VMEM((2, tg, 2, rhs, ts), F32),
            pltpu.VMEM((mg, 2, rhs, EDGE), BF16),
            pltpu.VMEM((mg, 2, rhs, EDGE), BF16),
            pltpu.VMEM((mg, 2, rhs, EDGE), BF16),
            pltpu.VMEM((mg, 2, rhs, EDGE), BF16),
            dma((nd - 1,)),
            dma((nd - 1,)),
            dma,
            dma((sectors,)),
            dma((sectors,)),
            dma((sectors,)),
            dma((2,)),
            dma((2,)),
            dma((2,)),
            dma((2,)),
            dma((2 * sectors, paths)),
            dma((2 * sectors, paths)),
            dma((2,)),
            dma((2,)),
            dma((sectors,)),
            dma,
        ],
        compiler_params=pltpu.CompilerParams(
            collective_id=0, has_side_effects=True, vmem_limit_bytes=63 * 1024 * 1024
        ),
    )(
        child,
        rank,
        fine_pattern,
        fine_interp,
        mid_interp,
        translator,
        fine_angle,
        top_angle,
        place[:fg],
        place[fg:],
        cnt,
    )


def solution(mesh):
    placed = (
        P(("box", "dir"), None, None, None),
        P("dir", None, None),
        P("dir", None, None),
        P(None, "dir"),
        P(None, "dir"),
        P(None, None, "dir"),
        P(),
        P(),
        P(),
        P(),
        P(),
        P(),
        P(),
    )
    return jax.shard_map(
        per_device,
        mesh=mesh,
        in_specs=placed,
        out_specs=(P("box", None, None, "dir"), P("box", None, None, "dir")),
        check_vma=False,
    )
```

```python
import functools

import jax
import jax.numpy as jnp
from jax import lax
from jax.experimental import pallas as pl
from jax.experimental.pallas import tpu as pltpu
from jax.sharding import PartitionSpec as P

MESH = pl.DeviceIdType.MESH
F32 = jnp.float32
BF16 = jnp.bfloat16
EDGE = 128


def visit_order(sectors):
    if sectors <= 2:
        return list(range(sectors))
    return [1, 0, sectors - 1] + list(range(2, sectors - 1))


def circle(angle):
    quarter = angle * 0.25
    x = quarter * quarter
    sine = quarter * (
        1.0 + x * (-1.0 / 6 + x * (1.0 / 120 + x * (-1.0 / 5040 + x * (1.0 / 362880))))
    )
    cosine = 1.0 + x * (
        -0.5 + x * (1.0 / 24 + x * (-1.0 / 720 + x * (1.0 / 40320 - x * (1.0 / 3628800))))
    )
    for _ in range(2):
        sine, cosine = 2.0 * sine * cosine, 1.0 - 2.0 * sine * sine
    return cosine, sine


def kernel(
    child,
    rank,
    fine,
    fint,
    mint,
    trans,
    fang,
    tang,
    fpos,
    mpos,
    cnt,
    top_out,
    mid_out,
    fcos,
    fsin,
    tcos,
    tsin,
    xf,
    fhl,
    fhr,
    wf,
    wm,
    xm,
    mhl,
    mhr,
    xs,
    gat,
    traw,
    tview,
    cpl,
    turned,
    raised,
    spread,
    acc,
    stage,
    esl,
    esr,
    erl,
    err,
    a2a_send,
    a2a_recv,
    own_sem,
    wf_sem,
    wm_sem,
    tr_sem,
    fh_send,
    fh_recv,
    mh_send,
    mh_recv,
    g_send,
    g_recv,
    ed_send,
    ed_recv,
    out_sem,
    mid_sem,
):
    nd = lax.axis_size("dir")
    nb = lax.axis_size("box")
    me = lax.axis_index("dir")
    box = lax.axis_index("box")
    chips = nb // 2
    sectors, kf, ms = fint.shape
    km, ts = mint.shape[1:]
    fl, _, rhs, fdir = fine.shape
    fg, _, _, fblock = xf.shape
    fs = fblock // sectors
    halo = (kf - fs) // 2
    mg = xm.shape[0]
    tg = mg // 4
    nt = tg * nb
    rows = 2 * rhs
    pad = EDGE - halo
    spanf = fs + 2 * EDGE
    spanm = ms + 2 * EDGE
    left = lax.rem(me + nd - 1, nd)
    right = lax.rem(me + 1, nd)
    sib = box + 1 - 2 * lax.rem(box, 2)
    across = [lax.rem(box + 2 * k, nb) for k in range(1, chips)]
    peers = [lax.rem(me + k, nd) for k in range(1, nd)]

    barrier = pltpu.get_barrier_semaphore()
    for p in peers:
        pl.semaphore_signal(barrier, inc=1, device_id={"dir": p}, device_id_type=MESH)
    for p in [sib] + across:
        pl.semaphore_signal(barrier, inc=1, device_id={"box": p}, device_id_type=MESH)
    pl.semaphore_wait(barrier, len(peers) + 1 + len(across))

    def columns(d):
        return pl.ds(pl.multiple_of(d * fblock, 128), fblock)

    mine = pl.ds(me * fl, fl)
    a2a = [
        pltpu.make_async_remote_copy(
            src_ref=fine.at[:, :, :, columns(p)],
            dst_ref=xf.at[mine],
            send_sem=a2a_send.at[k],
            recv_sem=a2a_recv.at[k],
            device_id={"dir": p},
            device_id_type=MESH,
        )
        for k, p in enumerate(peers)
    ]
    for c in a2a:
        c.start()
    own = pltpu.make_async_copy(fine.at[:, :, :, columns(me)], xf.at[mine], own_sem)
    own.start()

    wf_copies = [
        pltpu.make_async_copy(fint.at[s], wf.at[s, pl.ds(pad, kf)], wf_sem.at[s])
        for s in range(sectors)
    ]
    wm_copies = [
        pltpu.make_async_copy(mint.at[s], wm.at[s, pl.ds(pad, km)], wm_sem.at[s])
        for s in range(sectors)
    ]
    for c in wf_copies + wm_copies:
        c.start()

    for s in range(sectors):
        for buf, k, n in ((wf, kf, ms), (wm, km, ts)):
            buf[s, pl.ds(0, pad), :] = jnp.zeros((pad, n), BF16)
            buf[s, pl.ds(pad + k, pad), :] = jnp.zeros((pad, n), BF16)
    acc[...] = jnp.zeros(acc.shape, F32)

    kinds = trans.shape[0]
    for s in range(sectors):
        fetch = pltpu.make_async_copy(
            trans.at[:, :, pl.ds(s * ts, ts)], traw, tr_sem.at[s]
        )
        fetch.start()
        fetch.wait()

        @pl.loop(0, kinds // 8)
        def _(g, s=s):
            group = [traw[g * 8 + i].astype(F32) for i in range(8)]
            tview[
                pl.ds(pl.multiple_of(g * 16, 16), 16), pl.ds(s * ts, ts)
            ] = jnp.concatenate(group, axis=0).astype(BF16)

    for angles, places, cosines, sines, width in (
        (fang, fpos, fcos, fsin, 128),
        (tang, mpos, tcos, tsin, 256),
    ):

        @pl.loop(0, angles.shape[1] // width)
        def _(n, angles=angles, places=places, cosines=cosines, sines=sines, width=width):
            here = pl.ds(pl.multiple_of(n * width, width), width)
            table = angles[:, here]
            place = jnp.broadcast_to(places[...], (places.shape[0], width))
            angle = jnp.zeros(place.shape, F32)
            for p in range(table.shape[0]):
                row = jnp.broadcast_to(table[p : p + 1], place.shape)
                angle = jnp.where(place == p, row, angle)
            cosine, sine = circle(angle)
            cosines[:, here] = cosine
            sines[:, here] = sine

    own.wait()
    for c in a2a:
        c.wait_recv()

    def neighbour_copies(src_l, src_r, dst_l, dst_r, send, recv):
        return [
            pltpu.make_async_remote_copy(
                src_ref=src_r,
                dst_ref=dst_l,
                send_sem=send.at[0],
                recv_sem=recv.at[0],
                device_id={"dir": right},
                device_id_type=MESH,
            ),
            pltpu.make_async_remote_copy(
                src_ref=src_l,
                dst_ref=dst_r,
                send_sem=send.at[1],
                recv_sem=recv.at[1],
                device_id={"dir": left},
                device_id_type=MESH,
            ),
        ]

    fine_edges = neighbour_copies(
        xf.at[:, :, :, pl.ds(0, EDGE)],
        xf.at[:, :, :, pl.ds(fblock - EDGE, EDGE)],
        fhl,
        fhr,
        fh_send,
        fh_recv,
    )
    for c in fine_edges:
        c.start()

    def window(core, low, high, index, s, width):
        begin = s * width - EDGE
        end = (s + 1) * width + EDGE
        total = core.shape[3]
        parts = []
        if begin < 0:
            parts.append(low[index])
        first, last = max(begin, 0), min(end, total)
        parts.append(core[index, :, :, pl.ds(first, last - first)])
        if end > total:
            parts.append(high[index])
        parts = [p.reshape(rows, p.shape[-1]) for p in parts]
        return parts[0] if len(parts) == 1 else jnp.concatenate(parts, axis=1)

    group = 2 if mg % 2 == 0 else 1
    halo_seen = False
    for s in visit_order(sectors):
        if (s == 0 or s == sectors - 1) and not halo_seen:
            for c in fine_edges:
                c.wait_recv()
            halo_seen = True
        wf_copies[s].wait()

        @pl.loop(0, mg // group)
        def _(g, s=s):
            begin = g * 4 * group
            gathered = jnp.concatenate(
                [window(xf, fhl, fhr, child[begin + i], s, fs) for i in range(4 * group)], axis=0
            )
            coarse = jnp.dot(gathered, wf[s], preferred_element_type=F32)
            coarse = coarse.astype(BF16).astype(F32)
            for h in range(group):
                re = im = None
                for i in range(4 * h, 4 * h + 4):
                    turn = pl.ds(begin + i, 1)
                    c = fcos[turn, pl.ds(s * ms, ms)]
                    d = fsin[turn, pl.ds(s * ms, ms)]
                    u = coarse[i * rows : i * rows + rhs]
                    v = coarse[i * rows + rhs : (i + 1) * rows]
                    a, b = c * u - d * v, d * u + c * v
                    re, im = (a, b) if re is None else (re + a, im + b)
                xm[g * group + h, 0, :, pl.ds(s * ms, ms)] = re.astype(BF16)
                xm[g * group + h, 1, :, pl.ds(s * ms, ms)] = im.astype(BF16)

    mblock = sectors * ms
    mid_edges = neighbour_copies(
        xm.at[:, :, :, pl.ds(0, EDGE)],
        xm.at[:, :, :, pl.ds(mblock - EDGE, EDGE)],
        mhl,
        mhr,
        mh_send,
        mh_recv,
    )
    for c in mid_edges:
        c.start()

    tile = 256 if ts % 256 == 0 else 128
    tiles = ts // tile

    block = 256 if (mg * rows) % 256 == 0 else rows
    first = (tiles + 1) // 2
    halves = [(0, first)] + ([(first, tiles)] if first < tiles else [])

    def exchange(s, h, origin, path, target):
        low, high = halves[h]
        block = gat.at[s, origin, :, :, :, pl.ds(low * tile, (high - low) * tile)]
        return pltpu.make_async_remote_copy(
            src_ref=block,
            dst_ref=block,
            send_sem=g_send.at[2 * s + h, path],
            recv_sem=g_recv.at[2 * s + h, path],
            device_id={"box": target},
            device_id_type=MESH,
        )

    def near(s, h):
        return exchange(s, h, box, 0, sib)

    def far(s, h, k):
        return exchange(s, h, box, 1 + k, across[k])

    def pass_on(s, h, k):
        return exchange(s, h, lax.rem(box + nb - 2 * (k + 1), nb), chips + k, sib)

    halo_seen = False
    for s in visit_order(sectors):
        if (s == 0 or s == sectors - 1) and not halo_seen:
            for c in mid_edges:
                c.wait_recv()
            halo_seen = True
        wm_copies[s].wait()

        @pl.loop(0, mg)
        def _(i, s=s):
            xs[pl.ds(pl.multiple_of(i * rows, rows), rows), :] = window(
                xm, mhl, mhr, child[fg + i], s, ms
            )

        for h in range(len(halves)):

            low, high = halves[h]
            part = pl.ds(low * tile, (high - low) * tile)

            @pl.loop(0, mg * rows // block)
            def _(g, s=s, part=part):
                chunk = pl.ds(pl.multiple_of(g * block, block), block)
                raised[chunk, pl.ds(0, part.size)] = jnp.dot(
                    xs[chunk, :], wm[s, :, part], preferred_element_type=F32
                ).astype(BF16)

            @pl.loop(low, high)
            def _(n, s=s, low=low):
                here = pl.ds(pl.multiple_of(n * tile, tile), tile)
                whole = pl.ds(pl.multiple_of(s * ts + n * tile, 128), tile)
                there = pl.ds(pl.multiple_of((n - low) * tile, tile), tile)
                for t in range(tg):
                    re = im = None
                    for j in range(4):
                        i = t * 4 + j
                        turn = pl.ds(i, 1)
                        c = tcos[turn, whole]
                        d = tsin[turn, whole]
                        u = raised[pl.ds(i * rows, rhs), there].astype(F32)
                        v = raised[pl.ds(i * rows + rhs, rhs), there].astype(F32)
                        a, b = c * u - d * v, d * u + c * v
                        re, im = (a, b) if re is None else (re + a, im + b)
                    gat[s, box, t, 0, :, here] = re.astype(BF16)
                    gat[s, box, t, 1, :, here] = im.astype(BF16)

            for k in range(chips - 1):
                far(s, h, k).start()
            near(s, h).start()

    order = visit_order(sectors)
    edge_copies = neighbour_copies(esl, esr, erl, err, ed_send, ed_recv)
    out_copies = []
    depth = 384 if spanm % 384 == 0 else 128
    mfirst = rank.shape[0] - nb * mg + box * mg
    for step, s in enumerate(order):
        slot = step % 2
        if step >= 2:
            out_copies[step - 2].wait()
        for h in range(len(halves)):
            for k in range(chips - 1):
                far(s, h, k).wait_recv()
                pass_on(s, h, k).start()
            near(s, h).wait_recv()
            for k in range(chips - 1):
                pass_on(s, h, k).wait_recv()

            @pl.loop(*halves[h])
            def _(n, s=s, slot=slot):
                here = pl.ds(pl.multiple_of(n * tile, tile), tile)
                whole = pl.ds(pl.multiple_of(s * ts + n * tile, 128), tile)
                product = jnp.dot(cnt[...], tview[:, whole], preferred_element_type=F32)
                cpl[...] = product.astype(BF16).astype(F32)
                for t in range(tg):

                    def add(u, total, t=t):
                        re, im = total
                        origin = u // tg
                        q = u - origin * tg
                        c = cpl[pl.ds(2 * (t * nt + u), 1), :]
                        d = cpl[pl.ds(2 * (t * nt + u) + 1, 1), :]
                        a = gat[s, origin, q, 0, :, here].astype(F32)
                        b = gat[s, origin, q, 1, :, here].astype(F32)
                        return re + (c * a - d * b), im + (c * b + d * a)

                    total = (jnp.zeros((rhs, tile), F32), jnp.zeros((rhs, tile), F32))
                    if nt <= 8:
                        for u in range(nt):
                            total = add(u, total)
                    else:
                        total = lax.fori_loop(0, nt, add, total)
                    re, im = total
                    stage[slot, t, 0, :, here] = re
                    stage[slot, t, 1, :, here] = im
                    re = re.astype(BF16).astype(F32)
                    im = im.astype(BF16).astype(F32)
                    for j in range(4):
                        i = t * 4 + j
                        turn = pl.ds(i, 1)
                        c = tcos[turn, whole]
                        d = tsin[turn, whole]
                        turned[i, 0] = (c * re + d * im).astype(BF16)
                        turned[i, 1] = (c * im - d * re).astype(BF16)
                for m in range(mg):
                    spread[pl.ds(m * rows, rows), here] = turned[
                        rank[mfirst + m]
                    ].reshape(rows, tile)

        @pl.loop(0, spanm // depth)
        def _(n, s=s):
            back = pl.ds(pl.multiple_of(n * depth, depth), depth)
            target = pl.ds(pl.multiple_of(s * ms + n * depth, 128), depth)
            acc[:, :, :, target] += lax.dot_general(
                spread[...],
                wm[s, back, :],
                (((1,), (1,)), ((), ())),
                preferred_element_type=F32,
            ).reshape(mg, 2, rhs, depth)

        out = pltpu.make_async_copy(
            stage.at[slot],
            top_out.at[:, :, :, pl.ds(s * ts, ts)],
            out_sem.at[step],
        )
        out.start()
        out_copies.append(out)
        if set(order[: step + 1]) >= {0, sectors - 1} and not (
            set(order[:step]) >= {0, sectors - 1}
        ):
            esl[...] = acc[:, :, :, pl.ds(0, EDGE)].astype(BF16)
            esr[...] = acc[:, :, :, pl.ds(EDGE + mblock, EDGE)].astype(BF16)
            for c in edge_copies:
                c.start()

    for c in edge_copies:
        c.wait_recv()
    acc[:, :, :, pl.ds(EDGE, EDGE)] += erl[...].astype(F32)
    acc[:, :, :, pl.ds(mblock, EDGE)] += err[...].astype(F32)
    mid_copy = pltpu.make_async_copy(
        acc.at[:, :, :, pl.ds(EDGE, mblock)], mid_out, mid_sem
    )
    mid_copy.start()
    mid_copy.wait()

    for c in out_copies[-2:]:
        c.wait()
    for c in a2a + fine_edges + mid_edges + edge_copies:
        c.wait_send()
    for s in range(sectors):
        for h in range(len(halves)):
            near(s, h).wait_send()
            for k in range(chips - 1):
                far(s, h, k).wait_send()
                pass_on(s, h, k).wait_send()


def ranking(parents, wanted, positions):
    index = jnp.arange(parents.shape[0], dtype=jnp.int32)
    before = (parents[None, :] < parents[:, None]) | (
        (parents[None, :] == parents[:, None]) & (index[None, :] < index[:, None])
    )
    rank = jnp.sum(before.astype(jnp.int32), axis=1)
    chosen = (rank[None, :] == wanted[:, None]).astype(jnp.int32)
    child = jnp.sum(chosen * index[None, :], axis=1)
    return rank, child, jnp.sum(chosen * positions[None, :], axis=1, keepdims=True)


def pair_counts(pair_target, pair_source, pair_kind, base, targets, sources, kinds):
    place = jnp.arange(targets * sources * 2, dtype=jnp.int32)
    column = jnp.arange(kinds * 2, dtype=jnp.int32)
    inside = (pair_target >= base) & (pair_target < base + targets)
    slot = jnp.where(inside, (pair_target - base) * sources + pair_source, -1)
    in_slot = (slot[None, :] == (place // 2)[:, None]).astype(BF16)
    of_kind = (pair_kind[:, None] == (column // 2)[None, :]).astype(BF16)
    counts = jnp.dot(in_slot, of_kind, preferred_element_type=F32)
    same = (place % 2)[:, None] == (column % 2)[None, :]
    return jnp.where(same, counts, 0.0).astype(BF16)


def per_device(
    fine_pattern,
    fine_interp,
    mid_interp,
    fine_angle,
    top_angle,
    translator,
    fine_position,
    mid_position,
    fine_parent,
    mid_parent,
    pair_target,
    pair_source,
    pair_kind,
):
    box = lax.axis_index("box")
    nd = lax.axis_size("dir")
    nb = lax.axis_size("box")
    fl, _, rhs, fdir = fine_pattern.shape
    sectors, kf, ms = fine_interp.shape
    km, ts = mid_interp.shape[1:]
    kinds = translator.shape[0]
    fg = fl * nd
    mg = fg // 4
    tg = mg // 4
    nt = tg * nb
    rows = 2 * rhs
    fblock = fdir // nd
    fs = fblock // sectors
    mblock = sectors * ms
    tblock = sectors * ts
    chips = nb // 2
    tile = 256 if ts % 256 == 0 else 128

    fine_all = fine_parent.shape[0]
    slots = jnp.arange(fg + mg, dtype=jnp.int32)
    start = jnp.where(slots < fg, box * fg, fine_all + box * mg - fg)
    rank, child, place = ranking(
        jnp.concatenate([fine_parent, mid_parent + fine_all]),
        slots + start,
        jnp.concatenate([fine_position, mid_position]),
    )
    index = jnp.arange(rank.shape[0], dtype=jnp.int32)
    inner = jnp.where(index < fine_all, index % fg, (index - fine_all) % mg)
    rank = rank - (index - inner)
    child = child - jnp.where(slots < fg, box * fg, fine_all + box * mg)
    cnt = pair_counts(pair_target, pair_source, pair_kind, box * tg, tg, nt, kinds)

    vmem = pl.BlockSpec(memory_space=pltpu.VMEM)
    smem = pl.BlockSpec(memory_space=pltpu.SMEM)
    hbm = pl.BlockSpec(memory_space=pl.ANY)
    dma = pltpu.SemaphoreType.DMA
    paths = 2 * chips - 1
    return pl.pallas_call(
        kernel,
        out_shape=(
            jax.ShapeDtypeStruct((tg, 2, rhs, tblock), F32),
            jax.ShapeDtypeStruct((mg, 2, rhs, mblock), F32),
        ),
        in_specs=[smem] * 2 + [hbm] * 4 + [vmem] * 5,
        out_specs=(hbm, hbm),
        scratch_shapes=[
            pltpu.VMEM((fg, mblock), F32),
            pltpu.VMEM((fg, mblock), F32),
            pltpu.VMEM((mg, tblock), F32),
            pltpu.VMEM((mg, tblock), F32),
            pltpu.VMEM((fg, 2, rhs, fblock), BF16),
            pltpu.VMEM((fg, 2, rhs, EDGE), BF16),
            pltpu.VMEM((fg, 2, rhs, EDGE), BF16),
            pltpu.VMEM((sectors, fs + 2 * EDGE, ms), BF16),
            pltpu.VMEM((sectors, ms + 2 * EDGE, ts), BF16),
            pltpu.VMEM((mg, 2, rhs, mblock), BF16),
            pltpu.VMEM((mg, 2, rhs, EDGE), BF16),
            pltpu.VMEM((mg, 2, rhs, EDGE), BF16),
            pltpu.VMEM((mg * rows, ms + 2 * EDGE), BF16),
            pltpu.VMEM((sectors, nb, tg, 2, rhs, ts), BF16),
            pltpu.VMEM((kinds, 2, ts), BF16),
            pltpu.VMEM((2 * kinds, tblock), BF16),
            pltpu.VMEM((tg * nt * 2, tile), F32),
            pltpu.VMEM((mg, 2, rhs, tile), BF16),
            pltpu.VMEM((mg * rows, (ts // tile + 1) // 2 * tile), BF16),
            pltpu.VMEM((mg * rows, ts), BF16),
            pltpu.VMEM((mg, 2, rhs, mblock + 2 * EDGE), F32),
            pltpu.VMEM((2, tg, 2, rhs, ts), F32),
            pltpu.VMEM((mg, 2, rhs, EDGE), BF16),
            pltpu.VMEM((mg, 2, rhs, EDGE), BF16),
            pltpu.VMEM((mg, 2, rhs, EDGE), BF16),
            pltpu.VMEM((mg, 2, rhs, EDGE), BF16),
            dma((nd - 1,)),
            dma((nd - 1,)),
            dma,
            dma((sectors,)),
            dma((sectors,)),
            dma((sectors,)),
            dma((2,)),
            dma((2,)),
            dma((2,)),
            dma((2,)),
            dma((2 * sectors, paths)),
            dma((2 * sectors, paths)),
            dma((2,)),
            dma((2,)),
            dma((sectors,)),
            dma,
        ],
        compiler_params=pltpu.CompilerParams(
            collective_id=0, has_side_effects=True, vmem_limit_bytes=63 * 1024 * 1024
        ),
    )(
        child,
        rank,
        fine_pattern,
        fine_interp,
        mid_interp,
        translator,
        fine_angle,
        top_angle,
        place[:fg],
        place[fg:],
        cnt,
    )


def solution(mesh):
    placed = (
        P(("box", "dir"), None, None, None),
        P("dir", None, None),
        P("dir", None, None),
        P(None, "dir"),
        P(None, "dir"),
        P(None, None, "dir"),
        P(),
        P(),
        P(),
        P(),
        P(),
        P(),
        P(),
    )
    return jax.shard_map(
        per_device,
        mesh=mesh,
        in_specs=placed,
        out_specs=(P("box", None, None, "dir"), P("box", None, None, "dir")),
        check_vma=False,
    )
```

```python
import functools

import jax
import jax.numpy as jnp
from jax import lax
from jax.experimental import pallas as pl
from jax.experimental.pallas import tpu as pltpu
from jax.sharding import PartitionSpec as P

MESH = pl.DeviceIdType.MESH
F32 = jnp.float32
BF16 = jnp.bfloat16
EDGE = 128


def visit_order(sectors):
    if sectors <= 2:
        return list(range(sectors))
    return [1, 0, sectors - 1] + list(range(2, sectors - 1))


def circle(angle):
    quarter = angle * 0.25
    x = quarter * quarter
    sine = quarter * (
        1.0 + x * (-1.0 / 6 + x * (1.0 / 120 + x * (-1.0 / 5040 + x * (1.0 / 362880))))
    )
    cosine = 1.0 + x * (
        -0.5 + x * (1.0 / 24 + x * (-1.0 / 720 + x * (1.0 / 40320 - x * (1.0 / 3628800))))
    )
    for _ in range(2):
        sine, cosine = 2.0 * sine * cosine, 1.0 - 2.0 * sine * sine
    return cosine, sine


def kernel(
    child,
    rank,
    fine,
    fint,
    mint,
    trans,
    fang,
    tang,
    fpos,
    mpos,
    cnt,
    top_out,
    mid_out,
    fcos,
    fsin,
    tcos,
    tsin,
    xf,
    fhl,
    fhr,
    wf,
    wm,
    xm,
    mhl,
    mhr,
    xs,
    gat,
    traw,
    tview,
    cpl,
    turned,
    raised,
    spread,
    acc,
    stage,
    esl,
    esr,
    erl,
    err,
    a2a_send,
    a2a_recv,
    own_sem,
    wf_sem,
    wm_sem,
    tr_sem,
    fh_send,
    fh_recv,
    mh_send,
    mh_recv,
    g_send,
    g_recv,
    ed_send,
    ed_recv,
    out_sem,
    mid_sem,
):
    nd = lax.axis_size("dir")
    nb = lax.axis_size("box")
    me = lax.axis_index("dir")
    box = lax.axis_index("box")
    chips = nb // 2
    sectors, kf, ms = fint.shape
    km, ts = mint.shape[1:]
    fl, _, rhs, fdir = fine.shape
    fg, _, _, fblock = xf.shape
    fs = fblock // sectors
    halo = (kf - fs) // 2
    mg = xm.shape[0]
    tg = mg // 4
    nt = tg * nb
    rows = 2 * rhs
    pad = EDGE - halo
    spanf = fs + 2 * EDGE
    spanm = ms + 2 * EDGE
    left = lax.rem(me + nd - 1, nd)
    right = lax.rem(me + 1, nd)
    sib = box + 1 - 2 * lax.rem(box, 2)
    across = [lax.rem(box + 2 * k, nb) for k in range(1, chips)]
    peers = [lax.rem(me + k, nd) for k in range(1, nd)]

    barrier = pltpu.get_barrier_semaphore()
    for p in peers:
        pl.semaphore_signal(barrier, inc=1, device_id={"dir": p}, device_id_type=MESH)
    for p in [sib] + across:
        pl.semaphore_signal(barrier, inc=1, device_id={"box": p}, device_id_type=MESH)
    pl.semaphore_wait(barrier, len(peers) + 1 + len(across))

    def columns(d):
        return pl.ds(pl.multiple_of(d * fblock, 128), fblock)

    mine = pl.ds(me * fl, fl)
    a2a = [
        pltpu.make_async_remote_copy(
            src_ref=fine.at[:, :, :, columns(p)],
            dst_ref=xf.at[mine],
            send_sem=a2a_send.at[k],
            recv_sem=a2a_recv.at[k],
            device_id={"dir": p},
            device_id_type=MESH,
        )
        for k, p in enumerate(peers)
    ]
    for c in a2a:
        c.start()
    own = pltpu.make_async_copy(fine.at[:, :, :, columns(me)], xf.at[mine], own_sem)
    own.start()

    wf_copies = [
        pltpu.make_async_copy(fint.at[s], wf.at[s, pl.ds(pad, kf)], wf_sem.at[s])
        for s in range(sectors)
    ]
    wm_copies = [
        pltpu.make_async_copy(mint.at[s], wm.at[s, pl.ds(pad, km)], wm_sem.at[s])
        for s in range(sectors)
    ]
    for c in wf_copies + wm_copies:
        c.start()

    for s in range(sectors):
        for buf, k, n in ((wf, kf, ms), (wm, km, ts)):
            buf[s, pl.ds(0, pad), :] = jnp.zeros((pad, n), BF16)
            buf[s, pl.ds(pad + k, pad), :] = jnp.zeros((pad, n), BF16)
    acc[...] = jnp.zeros(acc.shape, F32)

    kinds = trans.shape[0]
    for s in range(sectors):
        fetch = pltpu.make_async_copy(
            trans.at[:, :, pl.ds(s * ts, ts)], traw, tr_sem.at[s]
        )
        fetch.start()
        fetch.wait()

        @pl.loop(0, kinds // 8)
        def _(g, s=s):
            group = [traw[g * 8 + i].astype(F32) for i in range(8)]
            tview[
                pl.ds(pl.multiple_of(g * 16, 16), 16), pl.ds(s * ts, ts)
            ] = jnp.concatenate(group, axis=0).astype(BF16)

    for angles, places, cosines, sines, width in (
        (fang, fpos, fcos, fsin, 128),
        (tang, mpos, tcos, tsin, 256),
    ):

        @pl.loop(0, angles.shape[1] // width)
        def _(n, angles=angles, places=places, cosines=cosines, sines=sines, width=width):
            here = pl.ds(pl.multiple_of(n * width, width), width)
            table = angles[:, here]
            place = jnp.broadcast_to(places[...], (places.shape[0], width))
            angle = jnp.zeros(place.shape, F32)
            for p in range(table.shape[0]):
                row = jnp.broadcast_to(table[p : p + 1], place.shape)
                angle = jnp.where(place == p, row, angle)
            cosine, sine = circle(angle)
            cosines[:, here] = cosine
            sines[:, here] = sine

    own.wait()
    for c in a2a:
        c.wait_recv()

    def neighbour_copies(src_l, src_r, dst_l, dst_r, send, recv):
        return [
            pltpu.make_async_remote_copy(
                src_ref=src_r,
                dst_ref=dst_l,
                send_sem=send.at[0],
                recv_sem=recv.at[0],
                device_id={"dir": right},
                device_id_type=MESH,
            ),
            pltpu.make_async_remote_copy(
                src_ref=src_l,
                dst_ref=dst_r,
                send_sem=send.at[1],
                recv_sem=recv.at[1],
                device_id={"dir": left},
                device_id_type=MESH,
            ),
        ]

    fine_edges = neighbour_copies(
        xf.at[:, :, :, pl.ds(0, EDGE)],
        xf.at[:, :, :, pl.ds(fblock - EDGE, EDGE)],
        fhl,
        fhr,
        fh_send,
        fh_recv,
    )
    for c in fine_edges:
        c.start()

    def window(core, low, high, index, s, width):
        begin = s * width - EDGE
        end = (s + 1) * width + EDGE
        total = core.shape[3]
        parts = []
        if begin < 0:
            parts.append(low[index])
        first, last = max(begin, 0), min(end, total)
        parts.append(core[index, :, :, pl.ds(first, last - first)])
        if end > total:
            parts.append(high[index])
        parts = [p.reshape(rows, p.shape[-1]) for p in parts]
        return parts[0] if len(parts) == 1 else jnp.concatenate(parts, axis=1)

    group = 2 if mg % 2 == 0 else 1
    halo_seen = False
    for s in visit_order(sectors):
        if (s == 0 or s == sectors - 1) and not halo_seen:
            for c in fine_edges:
                c.wait_recv()
            halo_seen = True
        wf_copies[s].wait()

        @pl.loop(0, mg // group)
        def _(g, s=s):
            begin = g * 4 * group
            gathered = jnp.concatenate(
                [window(xf, fhl, fhr, child[begin + i], s, fs) for i in range(4 * group)], axis=0
            )
            coarse = jnp.dot(gathered, wf[s], preferred_element_type=F32)
            coarse = coarse.astype(BF16).astype(F32)
            for h in range(group):
                re = im = None
                for i in range(4 * h, 4 * h + 4):
                    turn = pl.ds(begin + i, 1)
                    c = fcos[turn, pl.ds(s * ms, ms)]
                    d = fsin[turn, pl.ds(s * ms, ms)]
                    u = coarse[i * rows : i * rows + rhs]
                    v = coarse[i * rows + rhs : (i + 1) * rows]
                    a, b = c * u - d * v, d * u + c * v
                    re, im = (a, b) if re is None else (re + a, im + b)
                xm[g * group + h, 0, :, pl.ds(s * ms, ms)] = re.astype(BF16)
                xm[g * group + h, 1, :, pl.ds(s * ms, ms)] = im.astype(BF16)

    mblock = sectors * ms
    mid_edges = neighbour_copies(
        xm.at[:, :, :, pl.ds(0, EDGE)],
        xm.at[:, :, :, pl.ds(mblock - EDGE, EDGE)],
        mhl,
        mhr,
        mh_send,
        mh_recv,
    )
    for c in mid_edges:
        c.start()

    tile = 256 if ts % 256 == 0 else 128
    tiles = ts // tile

    block = 256 if (mg * rows) % 256 == 0 else rows
    first = (tiles + 1) // 2
    halves = [(0, first)] + ([(first, tiles)] if first < tiles else [])

    def exchange(s, h, origin, path, target):
        low, high = halves[h]
        block = gat.at[s, origin, :, :, :, pl.ds(low * tile, (high - low) * tile)]
        return pltpu.make_async_remote_copy(
            src_ref=block,
            dst_ref=block,
            send_sem=g_send.at[2 * s + h, path],
            recv_sem=g_recv.at[2 * s + h, path],
            device_id={"box": target},
            device_id_type=MESH,
        )

    def near(s, h):
        return exchange(s, h, box, 0, sib)

    def far(s, h, k):
        return exchange(s, h, box, 1 + k, across[k])

    def pass_on(s, h, k):
        return exchange(s, h, lax.rem(box + nb - 2 * (k + 1), nb), chips + k, sib)

    halo_seen = False
    for s in visit_order(sectors):
        if (s == 0 or s == sectors - 1) and not halo_seen:
            for c in mid_edges:
                c.wait_recv()
            halo_seen = True
        wm_copies[s].wait()

        @pl.loop(0, mg)
        def _(i, s=s):
            xs[pl.ds(pl.multiple_of(i * rows, rows), rows), :] = window(
                xm, mhl, mhr, child[fg + i], s, ms
            )

        for h in range(len(halves)):

            low, high = halves[h]
            part = pl.ds(low * tile, (high - low) * tile)

            @pl.loop(0, mg * rows // block)
            def _(g, s=s, part=part):
                chunk = pl.ds(pl.multiple_of(g * block, block), block)
                raised[chunk, pl.ds(0, part.size)] = jnp.dot(
                    xs[chunk, :], wm[s, :, part], preferred_element_type=F32
                ).astype(BF16)

            @pl.loop(low, high)
            def _(n, s=s, low=low):
                here = pl.ds(pl.multiple_of(n * tile, tile), tile)
                whole = pl.ds(pl.multiple_of(s * ts + n * tile, 128), tile)
                there = pl.ds(pl.multiple_of((n - low) * tile, tile), tile)
                for t in range(tg):
                    re = im = None
                    for j in range(4):
                        i = t * 4 + j
                        turn = pl.ds(i, 1)
                        c = tcos[turn, whole]
                        d = tsin[turn, whole]
                        u = raised[pl.ds(i * rows, rhs), there].astype(F32)
                        v = raised[pl.ds(i * rows + rhs, rhs), there].astype(F32)
                        a, b = c * u - d * v, d * u + c * v
                        re, im = (a, b) if re is None else (re + a, im + b)
                    gat[s, box, t, 0, :, here] = re.astype(BF16)
                    gat[s, box, t, 1, :, here] = im.astype(BF16)

            for k in range(chips - 1):
                far(s, h, k).start()
            near(s, h).start()

    order = visit_order(sectors)
    edge_copies = neighbour_copies(esl, esr, erl, err, ed_send, ed_recv)
    out_copies = []
    depth = 384 if spanm % 384 == 0 else 128
    mfirst = rank.shape[0] - nb * mg + box * mg
    for step, s in enumerate(order):
        slot = step % 2
        if step >= 2:
            out_copies[step - 2].wait()
        for h in range(len(halves)):
            for k in range(chips - 1):
                far(s, h, k).wait_recv()
                pass_on(s, h, k).start()
            near(s, h).wait_recv()
            for k in range(chips - 1):
                pass_on(s, h, k).wait_recv()

            @pl.loop(*halves[h])
            def _(n, s=s, slot=slot):
                here = pl.ds(pl.multiple_of(n * tile, tile), tile)
                whole = pl.ds(pl.multiple_of(s * ts + n * tile, 128), tile)
                product = jnp.dot(cnt[...], tview[:, whole], preferred_element_type=F32)
                cpl[...] = product.astype(BF16).astype(F32)

                def add(u, totals):
                    origin = u // tg
                    q = u - origin * tg
                    a = gat[s, origin, q, 0, :, here].astype(F32)
                    b = gat[s, origin, q, 1, :, here].astype(F32)
                    sums = []
                    for t in range(tg):
                        re, im = totals[t]
                        c = cpl[pl.ds(2 * (t * nt + u), 1), :]
                        d = cpl[pl.ds(2 * (t * nt + u) + 1, 1), :]
                        sums.append((re + (c * a - d * b), im + (c * b + d * a)))
                    return tuple(sums)

                nothing = jnp.zeros((rhs, tile), F32)
                totals = ((nothing, nothing),) * tg
                if nt <= 8:
                    for u in range(nt):
                        totals = add(u, totals)
                else:
                    totals = lax.fori_loop(0, nt, add, totals)
                for t in range(tg):
                    re, im = totals[t]
                    stage[slot, t, 0, :, here] = re
                    stage[slot, t, 1, :, here] = im
                    re = re.astype(BF16).astype(F32)
                    im = im.astype(BF16).astype(F32)
                    for j in range(4):
                        i = t * 4 + j
                        turn = pl.ds(i, 1)
                        c = tcos[turn, whole]
                        d = tsin[turn, whole]
                        turned[i, 0] = (c * re + d * im).astype(BF16)
                        turned[i, 1] = (c * im - d * re).astype(BF16)
                for m in range(mg):
                    spread[pl.ds(m * rows, rows), here] = turned[
                        rank[mfirst + m]
                    ].reshape(rows, tile)

        @pl.loop(0, spanm // depth)
        def _(n, s=s):
            back = pl.ds(pl.multiple_of(n * depth, depth), depth)
            target = pl.ds(pl.multiple_of(s * ms + n * depth, 128), depth)
            acc[:, :, :, target] += lax.dot_general(
                spread[...],
                wm[s, back, :],
                (((1,), (1,)), ((), ())),
                preferred_element_type=F32,
            ).reshape(mg, 2, rhs, depth)

        out = pltpu.make_async_copy(
            stage.at[slot],
            top_out.at[:, :, :, pl.ds(s * ts, ts)],
            out_sem.at[step],
        )
        out.start()
        out_copies.append(out)
        if set(order[: step + 1]) >= {0, sectors - 1} and not (
            set(order[:step]) >= {0, sectors - 1}
        ):
            esl[...] = acc[:, :, :, pl.ds(0, EDGE)].astype(BF16)
            esr[...] = acc[:, :, :, pl.ds(EDGE + mblock, EDGE)].astype(BF16)
            for c in edge_copies:
                c.start()

    for c in edge_copies:
        c.wait_recv()
    acc[:, :, :, pl.ds(EDGE, EDGE)] += erl[...].astype(F32)
    acc[:, :, :, pl.ds(mblock, EDGE)] += err[...].astype(F32)
    mid_copy = pltpu.make_async_copy(
        acc.at[:, :, :, pl.ds(EDGE, mblock)], mid_out, mid_sem
    )
    mid_copy.start()
    mid_copy.wait()

    for c in out_copies[-2:]:
        c.wait()
    for c in a2a + fine_edges + mid_edges + edge_copies:
        c.wait_send()
    for s in range(sectors):
        for h in range(len(halves)):
            near(s, h).wait_send()
            for k in range(chips - 1):
                far(s, h, k).wait_send()
                pass_on(s, h, k).wait_send()


def ranking(parents, wanted, positions):
    index = jnp.arange(parents.shape[0], dtype=jnp.int32)
    before = (parents[None, :] < parents[:, None]) | (
        (parents[None, :] == parents[:, None]) & (index[None, :] < index[:, None])
    )
    rank = jnp.sum(before.astype(jnp.int32), axis=1)
    chosen = (rank[None, :] == wanted[:, None]).astype(jnp.int32)
    child = jnp.sum(chosen * index[None, :], axis=1)
    return rank, child, jnp.sum(chosen * positions[None, :], axis=1, keepdims=True)


def pair_counts(pair_target, pair_source, pair_kind, base, targets, sources, kinds):
    place = jnp.arange(targets * sources * 2, dtype=jnp.int32)
    column = jnp.arange(kinds * 2, dtype=jnp.int32)
    inside = (pair_target >= base) & (pair_target < base + targets)
    slot = jnp.where(inside, (pair_target - base) * sources + pair_source, -1)
    in_slot = (slot[None, :] == (place // 2)[:, None]).astype(BF16)
    of_kind = (pair_kind[:, None] == (column // 2)[None, :]).astype(BF16)
    counts = jnp.dot(in_slot, of_kind, preferred_element_type=F32)
    same = (place % 2)[:, None] == (column % 2)[None, :]
    return jnp.where(same, counts, 0.0).astype(BF16)


def per_device(
    fine_pattern,
    fine_interp,
    mid_interp,
    fine_angle,
    top_angle,
    translator,
    fine_position,
    mid_position,
    fine_parent,
    mid_parent,
    pair_target,
    pair_source,
    pair_kind,
):
    box = lax.axis_index("box")
    nd = lax.axis_size("dir")
    nb = lax.axis_size("box")
    fl, _, rhs, fdir = fine_pattern.shape
    sectors, kf, ms = fine_interp.shape
    km, ts = mid_interp.shape[1:]
    kinds = translator.shape[0]
    fg = fl * nd
    mg = fg // 4
    tg = mg // 4
    nt = tg * nb
    rows = 2 * rhs
    fblock = fdir // nd
    fs = fblock // sectors
    mblock = sectors * ms
    tblock = sectors * ts
    chips = nb // 2
    tile = 256 if ts % 256 == 0 else 128

    fine_all = fine_parent.shape[0]
    slots = jnp.arange(fg + mg, dtype=jnp.int32)
    start = jnp.where(slots < fg, box * fg, fine_all + box * mg - fg)
    rank, child, place = ranking(
        jnp.concatenate([fine_parent, mid_parent + fine_all]),
        slots + start,
        jnp.concatenate([fine_position, mid_position]),
    )
    index = jnp.arange(rank.shape[0], dtype=jnp.int32)
    inner = jnp.where(index < fine_all, index % fg, (index - fine_all) % mg)
    rank = rank - (index - inner)
    child = child - jnp.where(slots < fg, box * fg, fine_all + box * mg)
    cnt = pair_counts(pair_target, pair_source, pair_kind, box * tg, tg, nt, kinds)

    vmem = pl.BlockSpec(memory_space=pltpu.VMEM)
    smem = pl.BlockSpec(memory_space=pltpu.SMEM)
    hbm = pl.BlockSpec(memory_space=pl.ANY)
    dma = pltpu.SemaphoreType.DMA
    paths = 2 * chips - 1
    return pl.pallas_call(
        kernel,
        out_shape=(
            jax.ShapeDtypeStruct((tg, 2, rhs, tblock), F32),
            jax.ShapeDtypeStruct((mg, 2, rhs, mblock), F32),
        ),
        in_specs=[smem] * 2 + [hbm] * 4 + [vmem] * 5,
        out_specs=(hbm, hbm),
        scratch_shapes=[
            pltpu.VMEM((fg, mblock), F32),
            pltpu.VMEM((fg, mblock), F32),
            pltpu.VMEM((mg, tblock), F32),
            pltpu.VMEM((mg, tblock), F32),
            pltpu.VMEM((fg, 2, rhs, fblock), BF16),
            pltpu.VMEM((fg, 2, rhs, EDGE), BF16),
            pltpu.VMEM((fg, 2, rhs, EDGE), BF16),
            pltpu.VMEM((sectors, fs + 2 * EDGE, ms), BF16),
            pltpu.VMEM((sectors, ms + 2 * EDGE, ts), BF16),
            pltpu.VMEM((mg, 2, rhs, mblock), BF16),
            pltpu.VMEM((mg, 2, rhs, EDGE), BF16),
            pltpu.VMEM((mg, 2, rhs, EDGE), BF16),
            pltpu.VMEM((mg * rows, ms + 2 * EDGE), BF16),
            pltpu.VMEM((sectors, nb, tg, 2, rhs, ts), BF16),
            pltpu.VMEM((kinds, 2, ts), BF16),
            pltpu.VMEM((2 * kinds, tblock), BF16),
            pltpu.VMEM((tg * nt * 2, tile), F32),
            pltpu.VMEM((mg, 2, rhs, tile), BF16),
            pltpu.VMEM((mg * rows, (ts // tile + 1) // 2 * tile), BF16),
            pltpu.VMEM((mg * rows, ts), BF16),
            pltpu.VMEM((mg, 2, rhs, mblock + 2 * EDGE), F32),
            pltpu.VMEM((2, tg, 2, rhs, ts), F32),
            pltpu.VMEM((mg, 2, rhs, EDGE), BF16),
            pltpu.VMEM((mg, 2, rhs, EDGE), BF16),
            pltpu.VMEM((mg, 2, rhs, EDGE), BF16),
            pltpu.VMEM((mg, 2, rhs, EDGE), BF16),
            dma((nd - 1,)),
            dma((nd - 1,)),
            dma,
            dma((sectors,)),
            dma((sectors,)),
            dma((sectors,)),
            dma((2,)),
            dma((2,)),
            dma((2,)),
            dma((2,)),
            dma((2 * sectors, paths)),
            dma((2 * sectors, paths)),
            dma((2,)),
            dma((2,)),
            dma((sectors,)),
            dma,
        ],
        compiler_params=pltpu.CompilerParams(
            collective_id=0, has_side_effects=True, vmem_limit_bytes=63 * 1024 * 1024
        ),
    )(
        child,
        rank,
        fine_pattern,
        fine_interp,
        mid_interp,
        translator,
        fine_angle,
        top_angle,
        place[:fg],
        place[fg:],
        cnt,
    )


def solution(mesh):
    placed = (
        P(("box", "dir"), None, None, None),
        P("dir", None, None),
        P("dir", None, None),
        P(None, "dir"),
        P(None, "dir"),
        P(None, None, "dir"),
        P(),
        P(),
        P(),
        P(),
        P(),
        P(),
        P(),
    )
    return jax.shard_map(
        per_device,
        mesh=mesh,
        in_specs=placed,
        out_specs=(P("box", None, None, "dir"), P("box", None, None, "dir")),
        check_vma=False,
    )
```
